32 devices in a mesh: tract: 2 (over y), patch: 4 (over z), band: 2 (over x), row: 2 (over core).
Axes of the slice: x: 2, y: 2, z: 4, core: 2. Of those that a mesh axis runs over, the one named last changes fastest.
Arguments:
- tiles: bfloat16 [4, 4, 32, 256, 256], P(('tract', 'band'), 'patch', None, 'row'), parts along dimension 0, may hold values from -6 to 6
- targets: int32 [4, 4, 32, 1], P(('tract', 'band'), 'patch'), parts along dimension 0, may hold values from 0 to 3; in each aligned block of 32 rows (0 to 31, 32 to 63, ..., all dimensions but the last counted through in order) at most 16 rows name the same one
- offsets: int32 [4, 4, 32, 2], P(('tract', 'band'), 'patch'), parts along dimension 0, may hold values from -4 to 4
- fractions: bfloat16 [4, 4, 32, 2], P(('tract', 'band'), 'patch'), parts along dimension 0, may hold values from 0 to 1
- kernels: bfloat16 [4, 4, 32, 2, 7], P(('tract', 'band'), 'patch'), parts along dimension 0, may hold values from 0.049804688 to 1
- weights: bfloat16 [4, 4, 32], P(('tract', 'band'), 'patch'), parts along dimension 0, may hold values from 0.25 to 4
- band_gain: float32 [2], replicated, may hold values from 0.5 to 2
Outputs:
- coadd: float32 [4, 4, 256, 256], P(('tract', 'band'), 'patch', 'row'), parts along dimension 0
- detection: float32 [8, 256, 256], P(('tract', 'patch'), ('row', 'band')), parts along dimension 0
- difference: bfloat16 [4, 4, 32, 256, 256], P(('tract', 'band'), 'patch', None, 'row'), parts along dimension 0
The draws below stay inside these ranges and needn't reach their ends.
There are 2 independent parts, one for each index of `tract`. The reference program is written for one: setup_inputs(seed, part) draws one part's arguments, and reference() takes and returns one part's arrays. A program takes and returns all parts, laid end to end along the dimension named above; an argument that names none is the same for every part. Nothing has to cross between parts.
Inputs may be any that keep to these rules, and one draw needn't show every extreme that they name: `targets`: among the 32 tiles of one device, at most 16 name the same patch, a bound that some block reaches of them.
All inputs are finite; a program needn't handle non-finite values.
Results may differ from the reference program's by a relative error of at most 0.013.
Values may be sent and summed in bfloat16 or wider, within the bound.
A program may use at most 128 MiB of HBM per device.

```python
import math
import jax
import jax.numpy as jnp
import numpy as np
from jax import lax

TS = 256
TILE_DEV = 32
PATCHES = 4
BANDS = 2
CAP = 16


def place_ends(entries, stream_key, smallest, largest):
    dims = entries.shape
    index_at = [jax.random.randint(jax.random.fold_in(stream_key, axis), (), 0, dims[axis]) for axis in range(len(dims))]
    entries = entries.at[tuple(index_at)].set(smallest)
    longest = dims.index(max(dims))
    index_at[longest] = (index_at[longest] + 1) % dims[longest]
    return entries.at[tuple(index_at)].set(largest)


def block_scale(own_key, shape, cuts, low, largest):
    factor_of, own = 1.0, jax.random.fold_in(own_key, 6)
    for axis_at, parts in cuts:
        heights = jnp.exp(jax.random.uniform(jax.random.fold_in(own, axis_at), (parts,), jnp.float32, low / len(cuts), largest / len(cuts)))
        factor_of = factor_of * jnp.repeat(heights, shape[axis_at] // parts).reshape([-1 if axis == axis_at else 1 for axis in range(len(shape))])
    return factor_of


def deal_out(key, own, number, rows, amount, top, most, slope):
    order = jax.random.permutation(key, amount)
    heavy_load, ordinary = portions_of(amount, rows * top, most, slope, True), portions_of(amount, rows * top, most, slope, False)
    places = jnp.arange(amount)

    def named(sizes, offset_by):
        used = int((sizes > 0).sum())
        fixed = max(1, used // 4)
        passed = fixed + (places - fixed + offset_by * (used - fixed)) % max(1, amount - fixed)
        return jnp.zeros((amount,), jnp.int32).at[order[jnp.where(places < fixed, places, passed)]].set(jnp.asarray(sizes, jnp.int32))

    sizes = jnp.where(number % 4 == 0, named(heavy_load, number // 4), named(ordinary, number - number // 4 - 1))
    mixed = jax.random.permutation(jax.random.fold_in(own, 3), amount)
    giver, receiver = mixed[0:amount // 2 * 2:2], mixed[1:amount // 2 * 2:2]
    slack = jnp.minimum(sizes[giver] - 1, most - sizes[receiver]) // 2
    slack = jnp.where((giver == order[0]) | (receiver == order[0]) | (sizes[receiver] == 0), 0, jnp.maximum(slack, 0))
    passed = jax.random.randint(jax.random.fold_in(own, 4), (amount // 2,), 0, 1 << 20) % (slack + 1)
    sizes = sizes.at[giver].add(-passed).at[receiver].add(passed)
    labels = jnp.searchsorted(jnp.cumsum(sizes), jnp.arange(rows * top), side="right").astype(jnp.int32)
    table = labels.reshape(top, rows).T
    table = table[jax.random.permutation(jax.random.fold_in(own, 1), rows)]
    offset_by = jax.random.randint(jax.random.fold_in(own, 2), (rows, 1), 0, top)
    return jnp.take_along_axis(table, (jnp.arange(top)[None, :] + offset_by) % top, axis=1)


def portions_of(count, total, most, skew, full):
    weights = [(1 << 20) // math.isqrt(grade ** skew) + 1 for grade in range(1, count + 1)]
    largest = most if full else min(most, max(-(-total // count), total * weights[0] // sum(weights)))
    least = 1 if total - largest >= count - 1 else 0
    given, surplus = [largest] + [least] * (count - 1), total - largest - least * (count - 1)
    while surplus > 0:
        free = [i for i in range(1, count) if given[i] < largest] or [i for i in range(1, count) if given[i] < most]
        pool, left = sum([weights[i] for i in free]), surplus
        for i in free:
            more = min(most - given[i], max(1, left * weights[i] // pool), surplus)
            given[i] = given[i] + more
            surplus = surplus - more
    return np.array(given)


def scatter_about(key, dims, width, most, pieces=(), kind=jnp.bfloat16):
    values = jax.random.normal(key, dims, jnp.float32) * width
    if len(pieces) > 0:
        values = block_scale(key, dims, pieces, -0.22, 0.18) * values
    return jnp.clip(values, min=-most, max=most).astype(kind)


def setup_inputs(seed: int = 0, part: int = 0) -> dict:
    streams_of = jax.random.split(jax.random.key(seed), 8)
    own_keys = jax.random.split(jax.random.fold_in(streams_of[7], part), 8)
    tiles = scatter_about(own_keys[0], (BANDS, PATCHES, TILE_DEV, TS, TS), 1.0, 6.0, ((0, 2), (1, 4), (3, 2)))
    targets_keys = jax.random.split(jax.random.fold_in(own_keys[1], 1), BANDS * PATCHES * TILE_DEV // TILE_DEV)
    targets_turns = jax.random.permutation(jax.random.fold_in(own_keys[1], 3), BANDS * PATCHES * TILE_DEV // TILE_DEV)
    targets = jax.vmap(lambda own, number: deal_out(jax.random.fold_in(own_keys[1], 2), own, number, TILE_DEV, PATCHES, 1, CAP, 2))(targets_keys, targets_turns).reshape((BANDS, PATCHES, TILE_DEV, 1))
    offsets = place_ends(jax.random.randint(own_keys[2], (BANDS, PATCHES, TILE_DEV, 2), -4, 5), jax.random.fold_in(own_keys[2], 1), -4, 4).astype(jnp.int32)
    fractions = jnp.clip(1.0 * jax.random.uniform(own_keys[3], (BANDS, PATCHES, TILE_DEV, 2), jnp.float32) ** block_scale(own_keys[3], (BANDS, PATCHES, TILE_DEV, 2), ((0, 2), (1, 4)), -0.2, 0.2), 0.0, 1.0).astype(jnp.bfloat16)
    kernels = jnp.clip(0.049804688 + 0.9501953 * jax.random.uniform(own_keys[4], (BANDS, PATCHES, TILE_DEV, 2, 7), jnp.float32) ** block_scale(own_keys[4], (BANDS, PATCHES, TILE_DEV, 2, 7), ((0, 2), (1, 4)), -0.2, 0.2), 0.049804688, 1.0).astype(jnp.bfloat16)
    weights = jnp.clip(jnp.exp(math.log(4.0) - 2.7725887 * jax.random.uniform(own_keys[5], (BANDS, PATCHES, TILE_DEV), jnp.float32) ** block_scale(own_keys[5], (BANDS, PATCHES, TILE_DEV), ((0, 2), (1, 4)), -0.2, 0.2)), 0.25, 4.0).astype(jnp.bfloat16)
    band_gain = jnp.clip(jax.random.uniform(streams_of[6], (BANDS,), jnp.float32, 0.5, 2.0), 0.5, 2.0)
    return dict(tiles=tiles, targets=targets, offsets=offsets, fractions=fractions, kernels=kernels, weights=weights, band_gain=band_gain)


reach = 11


def lanczos(value):
    return jnp.where(jnp.abs(value) < 3.0, jnp.sinc(value) * jnp.sinc(value / 3.0), 0.0)


def band_weights(rows, shifts, kernel_taps, extent):
    lag_values = jnp.arange(-reach - 3, reach + 4).astype(jnp.float32)
    lanczos_table = lanczos(lag_values[None, :] - shifts[:, None])
    result = jnp.zeros((shifts.shape[0], rows.shape[0], 2 * reach + 1), jnp.float32)
    for number in range(7):
        offset = number - 3
        inside = ((rows + offset >= 0) & (rows + offset < extent)).astype(jnp.float32)
        scaled = kernel_taps[:, number][:, None] * inside[None, :]
        result = result + scaled[:, :, None] * lanczos_table[:, None, 3 - offset:3 - offset + 2 * reach + 1]
    return result


def spread_full(band, rows, columns):
    lagged = columns[None, :] - rows[:, None]
    picker = jnp.clip(lagged + reach, 0, 2 * reach).astype(jnp.int32)
    picker = jnp.broadcast_to(picker[None], (band.shape[0],) + picker.shape)
    picked = jnp.take_along_axis(band, picker, axis=2)
    return jnp.where(jnp.abs(lagged)[None] <= reach, picked, 0.0)


def operators(shifts, kernel_taps, extent):
    rows = jnp.arange(extent).astype(jnp.int32)
    return spread_full(band_weights(rows, shifts, kernel_taps, extent), rows, rows).astype(jnp.bfloat16)


def reference(tiles, targets, offsets, fractions, kernels, weights, band_gain):
    extent = tiles.shape[-1]
    shifts = offsets.astype(jnp.float32) + fractions.astype(jnp.float32)
    taps = kernels.astype(jnp.float32)
    tile_weight = weights.astype(jnp.float32)

    def one_band(inputs):
        images_b, targets_b, shifts_b, taps_b, weights_b = inputs

        def add_group(carry, group):
            numer, denom = carry
            images, target, shift, tap, weight = group
            col_op = operators(shift[:, 0], tap[:, 0], extent)
            row_op = operators(shift[:, 1], tap[:, 1], extent)
            section = jnp.einsum('nrj,nij->nri', images.astype(jnp.float32), col_op.astype(jnp.float32)).astype(jnp.bfloat16)
            warped = jnp.einsum('nim,nmc->nic', row_op.astype(jnp.float32), section.astype(jnp.float32)).astype(jnp.bfloat16)
            chooser = (target[:, 0][:, None] == jnp.arange(PATCHES)[None, :]).astype(jnp.float32) * weight[:, None]
            partial_sum = jnp.einsum('tp,tij->pij', chooser, warped.astype(jnp.float32)).astype(jnp.bfloat16)
            partial_sum = lax.optimization_barrier(partial_sum)
            numer = numer + partial_sum.astype(jnp.float32)
            denom = denom + jnp.sum(chooser, axis=0)
            return (numer, denom), None

        start = (jnp.zeros((PATCHES, extent, extent), jnp.float32), jnp.zeros((PATCHES,), jnp.float32))
        (numer, denom), unused = lax.scan(add_group, start, (images_b, targets_b, shifts_b, taps_b, weights_b))
        return numer / (1.0 + denom)[:, None, None]

    coadd = lax.map(one_band, (tiles, targets, shifts, taps, tile_weight))
    detection = jnp.einsum('b,bpij->pij', band_gain, coadd, precision=lax.Precision.HIGHEST)
    coadd_low = coadd.astype(jnp.bfloat16)

    def band_difference(inputs):
        images_b, targets_b, shifts_b, taps_b, low_b = inputs

        def one_group(group):
            images, target, shift, tap = group
            chosen = low_b[target[:, 0]]
            col_op = operators(shift[:, 0], tap[:, 0], extent)
            row_op = operators(shift[:, 1], tap[:, 1], extent)
            back = jnp.einsum('nij,nic->njc', row_op.astype(jnp.float32), chosen.astype(jnp.float32)).astype(jnp.bfloat16)
            template = jnp.einsum('nji,nic->njc', back.astype(jnp.float32), col_op.astype(jnp.float32)).astype(jnp.bfloat16)
            return (images.astype(jnp.float32) - template.astype(jnp.float32)).astype(jnp.bfloat16)

        return lax.map(one_group, (images_b, targets_b, shifts_b, taps_b))

    difference = lax.map(band_difference, (tiles, targets, shifts, taps, coadd_low))
    return coadd, detection, difference
```

```python
import functools
import math

import jax
import jax.numpy as jnp
from jax import lax
from jax.experimental import pallas as pl
from jax.experimental.pallas import tpu as pltpu
from jax.sharding import PartitionSpec as P

EDGE = 16
MESH = pl.DeviceIdType.MESH


def lanczos(x):
    w = (x * x) * jnp.float32((math.pi / 3.0) ** 2)
    q = jnp.full_like(w, (-1.0) ** 10 / math.factorial(21))
    for k in range(9, -1, -1):
        q = q * w + jnp.float32((-1.0) ** k / math.factorial(2 * k + 1))
    q2 = q * q
    value = q2 * (1.0 - jnp.float32(4.0 / 3.0) * w * q2)
    return jnp.where(jnp.abs(x) < 3.0, value, 0.0)


def skewed(shift, taps):
    row = lax.broadcasted_iota(jnp.int32, (8, 128), 0)
    lane = lax.broadcasted_iota(jnp.int32, (8, 128), 1)
    lag = (lane - 64 - row).astype(jnp.float32)
    table = lanczos(lag - shift)
    mid = top = bottom = None
    for d in range(-3, 4):
        term = taps(d + 3) * (table if d == 0 else pltpu.roll(table, d % 128, 1))
        term_top = term if d >= 0 else jnp.where(row + d >= 0, term, 0.0)
        term_bottom = term if d <= 0 else jnp.where(row + d < 8, term, 0.0)
        mid = term if mid is None else mid + term
        top = term_top if top is None else top + term_top
        bottom = term_bottom if bottom is None else bottom + term_bottom
    return top, mid, bottom


def place(block, k):
    amount = (8 * k - 64) % 128
    return block if amount == 0 else pltpu.roll(block, amount, 1)


def low_half(block):
    lane = lax.broadcasted_iota(jnp.int32, block.shape, 1)
    return jnp.where(lane < 64, block, 0.0)


def high_half(block):
    lane = lax.broadcasted_iota(jnp.int32, block.shape, 1)
    return jnp.where(lane >= 64, block, 0.0)


def pair(first, second):
    return jnp.concatenate([first, second], axis=0).astype(jnp.bfloat16)


def build_columns(params_ref, t, put):
    top, mid, bottom = skewed(params_ref[t, 0], lambda d: params_ref[t, 2 + d])
    rolled = [place(mid, k) for k in range(16)]
    blocks = rolled + rolled
    blocks[0], blocks[31] = place(top, 0), place(bottom, 31)
    for q in range(16):
        both = blocks[2 * q], blocks[2 * q + 1]
        if q <= 8:
            f = low_half if q in (0, 8) else (high_half if q == 7 else (lambda b: b))
            left = [high_half(b) for b in both] if q in (7, 8) else [f(b) for b in both]
            put(q, 0, pair(*left))
        if q >= 7:
            if q in (7, 8):
                right = [low_half(b) for b in both]
            elif q == 15:
                right = [high_half(b) for b in both]
            else:
                right = both
            put(q, 1, pair(*right))


def build_rows(params_ref, t, side, scale, put):
    top, mid, bottom = skewed(params_ref[t, 1], lambda d: params_ref[t, 9 + d])
    if scale is not None:
        top, mid, bottom = top * scale, mid * scale, bottom * scale
    upper = side == 0
    first = jnp.where(upper, top, mid)
    last = jnp.where(upper, mid, bottom)
    blocks = [place(first, 0)] + [place(mid, k) for k in range(1, 15)] + [place(last, 15)]
    for q in range(8):
        both = blocks[2 * q], blocks[2 * q + 1]
        if q == 0:
            both = [low_half(b) for b in both]
        if q == 7:
            both = [high_half(b) for b in both]
        put(q, pair(*both))
    below = [high_half(place(mid, 16 + h)) for h in range(2)]
    above = [low_half(place(mid, h - 2)) for h in range(2)]
    put(8, pair(*[jnp.where(upper, b, a) for b, a in zip(below, above)]))


def forward_kernel(
    patches, group, params_ref, targets_ref, tiles_ref, main_ref, edge_ref,
    cols_ref, rows_ref, section_ref, mask_ref, den_ref,
):
    step = pl.program_id(0)
    side = lax.axis_index("row")
    height = tiles_ref.shape[1]

    @pl.when(step == 0)
    def _():
        cols_ref[...] = jnp.zeros_like(cols_ref)
        den_ref[...] = jnp.zeros_like(den_ref)

    index = lax.broadcasted_iota(jnp.int32, den_ref.shape, 0)
    for g in range(group):
        t = step * group + g
        weight = params_ref[t, 16]

        def put_col(q, half, tile):
            cols_ref[g, 16 * q : 16 * q + 16, 128 * half : 128 * half + 128] = tile

        def put_row(q, tile):
            rows_ref[16 * q : 16 * q + 16, pl.ds(pl.multiple_of(t * 128, 128), 128)] = tile

        build_columns(params_ref, t, put_col)
        build_rows(params_ref, t, side, weight, put_row)
        section = lax.dot_general(
            tiles_ref[g], cols_ref[g], (((1,), (1,)), ((), ())), preferred_element_type=jnp.float32
        )
        section_ref[pl.ds(pl.multiple_of(t * height, height), height), :] = section.astype(jnp.bfloat16)
        chosen = index == targets_ref[t, 0]
        mask_ref[:, pl.ds(pl.multiple_of(t * 128, 128), 128)] = jnp.where(chosen, 1.0, 0.0)
        den_ref[...] += jnp.where(chosen, weight, 0.0)

    @pl.when(step == pl.num_programs(0) - 1)
    def _():
        @pl.loop(0, patches)
        def _(p):
            mask = mask_ref[pl.ds(p, 1), :].astype(jnp.bfloat16)
            total = jnp.dot(
                rows_ref[...] * mask, section_ref[...], preferred_element_type=jnp.float32
            ).astype(jnp.bfloat16)
            main_ref[p, :height] = total[:height]
            edge_ref[p] = total[height:]
            den = den_ref[pl.ds(p, 1), :]
            den = jnp.concatenate([den, den], axis=1)
            high = den.astype(jnp.bfloat16).astype(jnp.float32)
            line = lax.broadcasted_iota(jnp.int32, (EDGE, 256), 0)
            parts = jnp.where(line == 0, high, jnp.where(line == 1, den - high, 0.0))
            main_ref[p, height:] = parts.astype(jnp.bfloat16)


def exchange_kernel(
    patches, bands, gain_ref, main_ref, edge_ref, coadd_ref, detection_ref, low_ref,
    main_in, edge_in, low_in, near_in, low_out, gained_out, gained_in,
    main_send, main_recv, edge_send, edge_recv, low_send, low_recv, near_send, near_recv,
    band_send, band_recv,
):
    me = lax.axis_index("patch")
    band = lax.axis_index("band")
    side = lax.axis_index("row")
    height, share = coadd_ref.shape[0], detection_ref.shape[0]
    across = 1 - side
    edge_at = pl.multiple_of((1 - side) * (height - EDGE), EDGE)

    barrier = pltpu.get_barrier_semaphore()
    others = [lax.rem(me + k, patches) for k in range(1, patches)]
    everyone = [me] + others
    partners = [lax.rem(band + k, bands) for k in range(1, bands)]
    for z in others:
        pl.semaphore_signal(barrier, inc=1, device_id={"patch": z}, device_id_type=MESH)
    for z in everyone:
        pl.semaphore_signal(
            barrier, inc=1, device_id={"patch": z, "row": across}, device_id_type=MESH
        )
    for b in partners:
        pl.semaphore_signal(barrier, inc=1, device_id={"band": b}, device_id_type=MESH)
    pl.semaphore_wait(barrier, 2 * patches - 1 + bands - 1)

    def remote(source, place_at, send, recv, where):
        return pltpu.make_async_remote_copy(
            src_ref=source, dst_ref=place_at, send_sem=send, recv_sem=recv,
            device_id=where, device_id_type=MESH,
        )

    copies = []
    for k in range(1, patches):
        z = lax.rem(me + k, patches)
        copies.append(remote(main_ref.at[z], main_in.at[k], main_send.at[k], main_recv.at[k], {"patch": z}))
    for k in range(patches):
        z = lax.rem(me + k, patches)
        copies.append(
            remote(edge_ref.at[z], edge_in.at[k], edge_send.at[k], edge_recv.at[k], {"patch": z, "row": across})
        )
    for copy in copies:
        copy.start()
    for copy in copies:
        copy.wait()

    total = main_ref[me].astype(jnp.float32)
    near = edge_in[0].astype(jnp.float32)
    for k in range(1, patches):
        total += main_in[k].astype(jnp.float32)
        near += edge_in[k].astype(jnp.float32)
    den = 1.0 + jnp.sum(total[height:], axis=0, keepdims=True)
    coadd_ref[...] = total[:height] / den
    coadd_ref[pl.ds(edge_at, EDGE), :] += near / den
    coadd = coadd_ref[...]
    low_out[...] = coadd.astype(jnp.bfloat16)
    gained = gain_ref[band] * coadd
    gained_out[...] = gained.astype(jnp.bfloat16)

    copies = []
    for k in range(1, patches):
        z = lax.rem(me + k, patches)
        copies.append(remote(low_out, low_in.at[k], low_send.at[k], low_recv.at[k], {"patch": z}))
    for k in range(patches):
        z = lax.rem(me + k, patches)
        copies.append(
            remote(
                low_out.at[pl.ds(edge_at, EDGE)], near_in.at[k], near_send.at[k], near_recv.at[k],
                {"patch": z, "row": across},
            )
        )
    for k in range(1, bands):
        b = lax.rem(band + k, bands)
        copies.append(
            remote(
                gained_out.at[pl.ds(pl.multiple_of(b * share, EDGE), share)], gained_in.at[k],
                band_send.at[k], band_recv.at[k], {"band": b},
            )
        )
    for copy in copies:
        copy.start()
    low_ref[me, :height] = low_out[...]
    for copy in copies:
        copy.wait()
    detection = gain_ref[band] * coadd_ref[pl.ds(pl.multiple_of(band * share, EDGE), share), :]
    for k in range(1, bands):
        detection += gained_in[k].astype(jnp.float32)
    detection_ref[...] = detection
    for k in range(patches):
        z = lax.rem(me - k + patches, patches)
        if k > 0:
            low_ref[z, :height] = low_in[k]
        low_ref[z, height:] = near_in[k]


def backward_kernel(group, params_ref, targets_ref, tiles_ref, low_ref, out_ref, cols_ref, rows_ref):
    step = pl.program_id(0)
    side = lax.axis_index("row")

    @pl.when(step == 0)
    def _():
        cols_ref[...] = jnp.zeros_like(cols_ref)

    for g in range(group):
        t = step * group + g

        def put_col(q, half, tile):
            cols_ref[g, 16 * q : 16 * q + 16, 128 * half : 128 * half + 128] = tile

        def put_row(q, tile):
            rows_ref[g, 16 * q : 16 * q + 16, :] = tile

        build_columns(params_ref, t, put_col)
        build_rows(params_ref, t, side, None, put_row)
        back = lax.dot_general(
            rows_ref[g], low_ref[targets_ref[t, 0]], (((0,), (0,)), ((), ())),
            preferred_element_type=jnp.float32,
        ).astype(jnp.bfloat16)
        template = jnp.dot(back, cols_ref[g], preferred_element_type=jnp.float32)
        template = template.astype(jnp.bfloat16).astype(jnp.float32)
        out_ref[g] = (tiles_ref[g].astype(jnp.float32) - template).astype(jnp.bfloat16)


def body(tiles, targets, offsets, fractions, kernels, weights, band_gain):
    holding, height, extent = tiles.shape[2:]
    patches, bands = lax.axis_size("patch"), lax.axis_size("band")
    images, target = tiles[0, 0], targets[0, 0]
    params = jnp.concatenate(
        [
            offsets[0, 0].astype(jnp.float32) + fractions[0, 0].astype(jnp.float32),
            kernels[0, 0].reshape(holding, 14).astype(jnp.float32),
            weights[0, 0][:, None].astype(jnp.float32),
        ],
        axis=1,
    )
    smem = pl.BlockSpec(memory_space=pltpu.SMEM)
    vmem = pl.BlockSpec(memory_space=pltpu.VMEM)
    group = 8
    padded = -(-patches // 8) * 8
    tile_spec = pl.BlockSpec((group, height, extent), lambda i: (i, 0, 0))
    whole = lambda *shape: pl.BlockSpec(shape, lambda i: (0,) * len(shape))
    macs = holding * height * extent * extent
    main, edge = pl.pallas_call(
        functools.partial(forward_kernel, patches, group),
        grid=(holding // group,),
        in_specs=[smem, smem, tile_spec],
        out_specs=[whole(patches, height + EDGE, extent), whole(patches, EDGE, extent)],
        out_shape=[
            jax.ShapeDtypeStruct((patches, height + EDGE, extent), jnp.bfloat16),
            jax.ShapeDtypeStruct((patches, EDGE, extent), jnp.bfloat16),
        ],
        scratch_shapes=[
            pltpu.VMEM((group, extent, extent), jnp.bfloat16),
            pltpu.VMEM((height + EDGE, holding * 128), jnp.bfloat16),
            pltpu.VMEM((holding * height, extent), jnp.bfloat16),
            pltpu.VMEM((padded, holding * 128), jnp.float32),
            pltpu.VMEM((padded, 128), jnp.float32),
        ],
        compiler_params=pltpu.CompilerParams(vmem_limit_bytes=40 << 20),
        cost_estimate=pl.CostEstimate(flops=2 * macs * 4, bytes_accessed=3 << 20, transcendentals=0),
        name="forward",
    )(params, target, images)

    share = height // bands
    dma = pltpu.SemaphoreType.DMA
    coadd, detection, low = pl.pallas_call(
        functools.partial(exchange_kernel, patches, bands),
        in_specs=[smem, vmem, vmem],
        out_specs=[vmem, vmem, vmem],
        out_shape=[
            jax.ShapeDtypeStruct((height, extent), jnp.float32),
            jax.ShapeDtypeStruct((share, extent), jnp.float32),
            jax.ShapeDtypeStruct((patches, height + EDGE, extent), jnp.bfloat16),
        ],
        scratch_shapes=[
            pltpu.VMEM((patches, height + EDGE, extent), jnp.bfloat16),
            pltpu.VMEM((patches, EDGE, extent), jnp.bfloat16),
            pltpu.VMEM((patches, height, extent), jnp.bfloat16),
            pltpu.VMEM((patches, EDGE, extent), jnp.bfloat16),
            pltpu.VMEM((height, extent), jnp.bfloat16),
            pltpu.VMEM((height, extent), jnp.bfloat16),
            pltpu.VMEM((bands, share, extent), jnp.bfloat16),
        ]
        + [dma((patches,))] * 8
        + [dma((bands,))] * 2,
        compiler_params=pltpu.CompilerParams(
            collective_id=0, has_side_effects=True, vmem_limit_bytes=40 << 20
        ),
        cost_estimate=pl.CostEstimate(flops=1 << 20, bytes_accessed=2 << 20, transcendentals=0),
        name="exchange",
    )(band_gain, main, edge)

    difference = pl.pallas_call(
        functools.partial(backward_kernel, group),
        grid=(holding // group,),
        in_specs=[smem, smem, tile_spec, whole(patches, height + EDGE, extent)],
        out_specs=tile_spec,
        out_shape=jax.ShapeDtypeStruct((holding, height, extent), jnp.bfloat16),
        scratch_shapes=[
            pltpu.VMEM((group, extent, extent), jnp.bfloat16),
            pltpu.VMEM((group, height + EDGE, 128), jnp.bfloat16),
        ],
        compiler_params=pltpu.CompilerParams(vmem_limit_bytes=40 << 20),
        cost_estimate=pl.CostEstimate(flops=4 * macs, bytes_accessed=5 << 20, transcendentals=0),
        name="backward",
    )(params, target, images, low)
    return (coadd[None, None], detection[None], difference[None, None])


def solution(mesh):
    placed = (
        P(("tract", "band"), "patch", None, "row", None),
        P(("tract", "band"), "patch", None, None),
        P(("tract", "band"), "patch", None, None),
        P(("tract", "band"), "patch", None, None),
        P(("tract", "band"), "patch", None, None, None),
        P(("tract", "band"), "patch", None),
        P(),
    )
    return jax.shard_map(
        body,
        mesh=mesh,
        in_specs=placed,
        out_specs=(
            P(("tract", "band"), "patch", "row", None),
            P(("tract", "patch"), ("row", "band"), None),
            P(("tract", "band"), "patch", None, "row", None),
        ),
        check_vma=False,
    )
```

```python
import functools
import math

import jax
import jax.numpy as jnp
from jax import lax
from jax.experimental import pallas as pl
from jax.experimental.pallas import tpu as pltpu
from jax.sharding import PartitionSpec as P

EDGE = 16
MESH = pl.DeviceIdType.MESH


def lanczos(x):
    w = (x * x) * jnp.float32((math.pi / 3.0) ** 2)
    q = jnp.full_like(w, (-1.0) ** 10 / math.factorial(21))
    for k in range(9, -1, -1):
        q = q * w + jnp.float32((-1.0) ** k / math.factorial(2 * k + 1))
    q2 = q * q
    value = q2 * (1.0 - jnp.float32(4.0 / 3.0) * w * q2)
    return jnp.where(jnp.abs(x) < 3.0, value, 0.0)


def skewed(shift, taps):
    row = lax.broadcasted_iota(jnp.int32, (8, 128), 0)
    lane = lax.broadcasted_iota(jnp.int32, (8, 128), 1)
    lag = (lane - 64 - row).astype(jnp.float32)
    table = lanczos(lag - shift)
    mid = top = bottom = None
    for d in range(-3, 4):
        term = taps(d + 3) * (table if d == 0 else pltpu.roll(table, d % 128, 1))
        term_top = term if d >= 0 else jnp.where(row + d >= 0, term, 0.0)
        term_bottom = term if d <= 0 else jnp.where(row + d < 8, term, 0.0)
        mid = term if mid is None else mid + term
        top = term_top if top is None else top + term_top
        bottom = term_bottom if bottom is None else bottom + term_bottom
    return top, mid, bottom


def place(block, k):
    amount = (8 * k - 64) % 128
    return block if amount == 0 else pltpu.roll(block, amount, 1)


def low_half(block):
    lane = lax.broadcasted_iota(jnp.int32, block.shape, 1)
    return jnp.where(lane < 64, block, 0.0)


def high_half(block):
    lane = lax.broadcasted_iota(jnp.int32, block.shape, 1)
    return jnp.where(lane >= 64, block, 0.0)


def pair(first, second):
    return jnp.concatenate([first, second], axis=0).astype(jnp.bfloat16)


def build_columns(params_ref, t, put):
    top, mid, bottom = skewed(params_ref[t, 0], lambda d: params_ref[t, 2 + d])
    rolled = [place(mid, k) for k in range(16)]
    blocks = rolled + rolled
    blocks[0], blocks[31] = place(top, 0), place(bottom, 31)
    zero = jnp.zeros((16, 128), jnp.bfloat16)
    for q in range(16):
        both = blocks[2 * q], blocks[2 * q + 1]
        if q > 8:
            put(q, 0, zero)
        elif q in (7, 8):
            put(q, 0, pair(*[high_half(b) for b in both]))
        else:
            put(q, 0, pair(*[low_half(b) if q == 0 else b for b in both]))
        if q < 7:
            put(q, 1, zero)
        elif q in (7, 8):
            put(q, 1, pair(*[low_half(b) for b in both]))
        else:
            put(q, 1, pair(*[high_half(b) if q == 15 else b for b in both]))


def build_rows(params_ref, t, side, scale, put):
    top, mid, bottom = skewed(params_ref[t, 1], lambda d: params_ref[t, 9 + d])
    top, mid, bottom = top * scale, mid * scale, bottom * scale
    upper = side == 0
    first = jnp.where(upper, top, mid)
    last = jnp.where(upper, mid, bottom)
    blocks = [place(first, 0)] + [place(mid, k) for k in range(1, 15)] + [place(last, 15)]
    for q in range(8):
        both = blocks[2 * q], blocks[2 * q + 1]
        if q == 0:
            both = [low_half(b) for b in both]
        if q == 7:
            both = [high_half(b) for b in both]
        put(q, pair(*both))
    below = [high_half(place(mid, 16 + h)) for h in range(2)]
    above = [low_half(place(mid, h - 2)) for h in range(2)]
    put(8, pair(*[jnp.where(upper, b, a) for b, a in zip(below, above)]))


def coadd_kernel(
    patches, bands, group, params_ref, targets_ref, gain_ref, tiles_hbm,
    coadd_ref, detection_ref, out_hbm,
    tiles_ref, diff_ref, cols_ref, rows_ref, turned_ref, section_ref, mask_ref, den_ref,
    near_out, edge_out, far_out, near_in, edge_in, far_in, low_ref, gained_out, gained_in,
    tile_sem, out_sem, near_send, near_recv, edge_send, edge_recv, far_send, far_recv,
    near_back_send, near_back_recv, edge_back_send, edge_back_recv, far_back_send, far_back_recv,
    band_send, band_recv,
):
    me = lax.axis_index("patch")
    band = lax.axis_index("band")
    side = lax.axis_index("row")
    holding, height = tiles_ref.shape[:2]
    share = detection_ref.shape[0]
    half = height // 2
    groups = holding // group
    across = 1 - side
    near_at = pl.multiple_of((1 - side) * half, EDGE)
    far_at = pl.multiple_of(side * half, EDGE)
    edge_at = pl.multiple_of((1 - side) * (half - EDGE), EDGE)

    def tile_copy(i):
        part = pl.ds(i * group, group)
        return pltpu.make_async_copy(tiles_hbm.at[part], tiles_ref.at[part], tile_sem.at[i])

    def out_copy(i):
        part = pl.ds(i * group, group)
        return pltpu.make_async_copy(diff_ref.at[part], out_hbm.at[part], out_sem.at[i])

    for i in range(groups):
        tile_copy(i).start()
    barrier = pltpu.get_barrier_semaphore()
    for k in range(1, patches):
        z = lax.rem(me + k, patches)
        pl.semaphore_signal(barrier, inc=1, device_id={"patch": z}, device_id_type=MESH)
    for k in range(patches):
        z = lax.rem(me + k, patches)
        pl.semaphore_signal(
            barrier, inc=1, device_id={"patch": z, "row": across}, device_id_type=MESH
        )
    for k in range(1, bands):
        b = lax.rem(band + k, bands)
        pl.semaphore_signal(barrier, inc=1, device_id={"band": b}, device_id_type=MESH)

    def remote(source, place_at, send, recv, where):
        return pltpu.make_async_remote_copy(
            src_ref=source, dst_ref=place_at, send_sem=send, recv_sem=recv,
            device_id=where, device_id_type=MESH,
        )

    den_ref[...] = jnp.zeros_like(den_ref)
    index = lax.broadcasted_iota(jnp.int32, den_ref.shape, 0)

    @pl.loop(0, groups)
    def _(i):
        tile_copy(i).wait()
        for g in range(group):
            t = i * group + g
            weight = params_ref[t, 16]
            lanes = pl.ds(pl.multiple_of(t * 128, 128), 128)

            def put_col(q, part, tile):
                cols_ref[t, 16 * q : 16 * q + 16, 128 * part : 128 * part + 128] = tile

            def put_row(q, tile):
                if q == 8:
                    start = half
                elif q < 4:
                    start = 16 * q + (1 - side) * (half + EDGE)
                else:
                    start = 16 * (q - 4) + side * (half + EDGE)
                rows_ref[pl.ds(pl.multiple_of(start, EDGE), EDGE), lanes] = tile

            build_columns(params_ref, t, put_col)
            build_rows(params_ref, t, side, weight, put_row)
            section = lax.dot_general(
                tiles_ref[t], cols_ref[t], (((1,), (1,)), ((), ())), preferred_element_type=jnp.float32
            )
            section_ref[pl.ds(pl.multiple_of(t * height, height), height), :] = section.astype(jnp.bfloat16)
            chosen = index == targets_ref[t, 0]
            mask_ref[:, lanes] = jnp.where(chosen, 1.0, 0.0)
            den_ref[...] += jnp.where(chosen, weight, 0.0)

    pl.semaphore_wait(barrier, 2 * patches - 1 + bands - 1)

    def near_copy(k):
        z = lax.rem(me + k, patches)
        return remote(near_out.at[k], near_in.at[k], near_send.at[k], near_recv.at[k], {"patch": z})

    def edge_copy(k):
        z = lax.rem(me + k, patches)
        return remote(
            edge_out.at[k], edge_in.at[k], edge_send.at[k], edge_recv.at[k], {"patch": z, "row": across}
        )

    def far_copy(k):
        z = lax.rem(me + k, patches)
        return remote(far_out.at[k], far_in.at[k], far_send.at[k], far_recv.at[k], {"patch": z})

    def patch_sum(z, start, size):
        mask = mask_ref[pl.ds(z, 1), :].astype(jnp.bfloat16)
        return jnp.dot(
            rows_ref[start : start + size] * mask, section_ref[...], preferred_element_type=jnp.float32
        ).astype(jnp.bfloat16)

    def near_sum(k):
        z = lax.rem(me + k, patches)
        total = patch_sum(z, 0, half + EDGE)
        near_out[k, :half] = total[:half]
        edge_out[k] = total[half:]
        den = den_ref[pl.ds(z, 1), :]
        den = jnp.concatenate([den, den], axis=1)
        high = den.astype(jnp.bfloat16).astype(jnp.float32)
        line = lax.broadcasted_iota(jnp.int32, (EDGE, 256), 0)
        parts = jnp.where(line == 0, high, jnp.where(line == 1, den - high, 0.0))
        near_out[k, half:] = parts.astype(jnp.bfloat16)

    @pl.loop(1, patches)
    def _(k):
        near_sum(k)
        near_copy(k).start()
        edge_copy(k).start()

    near_sum(0)
    edge_copy(0).start()

    @pl.loop(1, patches)
    def _(k):
        far_out[k] = patch_sum(lax.rem(me + k, patches), half + EDGE, half)
        far_copy(k).start()

    far_out[0] = patch_sum(me, half + EDGE, half)

    def turn(t):
        lanes = pl.ds(pl.multiple_of(t * 128, 128), 128)
        block = rows_ref[:, lanes].astype(jnp.float32) * (1.0 / params_ref[t, 16])
        turned_ref[t] = block.T.astype(jnp.bfloat16)

    @pl.loop(0, holding // 8)
    def _(i):
        for g in range(4):
            turn(i * 4 + g)

    for k in range(1, patches):
        near_copy(k).wait()
    for k in range(patches):
        edge_copy(k).wait()
    total = near_out[0].astype(jnp.float32)
    beside = edge_in[0].astype(jnp.float32)
    for k in range(1, patches):
        total += near_in[k].astype(jnp.float32)
        beside += edge_in[k].astype(jnp.float32)
    factor = 1.0 / (1.0 + jnp.sum(total[half:], axis=0, keepdims=True))
    zero = jnp.zeros((half - EDGE, 256), jnp.float32)
    beside = jnp.where(
        side == 0,
        jnp.concatenate([zero, beside], axis=0),
        jnp.concatenate([beside, zero], axis=0),
    )
    near = (total[:half] + beside) * factor
    low_ref[me, :half] = near.astype(jnp.bfloat16)

    def near_back(k):
        z = lax.rem(me + k, patches)
        here = low_ref.at[me, pl.ds(0, half)]
        return remote(here, here, near_back_send.at[k], near_back_recv.at[k], {"patch": z})

    def edge_back(k):
        z = lax.rem(me + k, patches)
        return remote(
            low_ref.at[me, pl.ds(edge_at, EDGE)], low_ref.at[me, pl.ds(half, EDGE)],
            edge_back_send.at[k], edge_back_recv.at[k], {"patch": z, "row": across},
        )

    def far_back(k):
        z = lax.rem(me + k, patches)
        here = low_ref.at[me, pl.ds(half + EDGE, half)]
        return remote(here, here, far_back_send.at[k], far_back_recv.at[k], {"patch": z})

    for k in range(1, patches):
        near_back(k).start()
    for k in range(patches):
        edge_back(k).start()
    coadd_ref[pl.ds(near_at, half), :] = near
    gained_out[pl.ds(near_at, half), :] = (gain_ref[band] * near).astype(jnp.bfloat16)

    for k in range(1, patches):
        far_copy(k).wait()
    far = far_out[0].astype(jnp.float32)
    for k in range(1, patches):
        far += far_in[k].astype(jnp.float32)
    far = far * factor
    low_ref[me, half + EDGE :] = far.astype(jnp.bfloat16)
    for k in range(1, patches):
        far_back(k).start()
    coadd_ref[pl.ds(far_at, half), :] = far
    gained_out[pl.ds(far_at, half), :] = (gain_ref[band] * far).astype(jnp.bfloat16)

    def band_copy(k):
        b = lax.rem(band + k, bands)
        return remote(
            gained_out.at[pl.ds(pl.multiple_of(b * share, EDGE), share)], gained_in.at[k],
            band_send.at[k], band_recv.at[k], {"band": b},
        )

    for k in range(1, bands):
        band_copy(k).start()

    @pl.loop(holding // 8, holding // 4)
    def _(i):
        for g in range(4):
            turn(i * 4 + g)

    for k in range(1, bands):
        band_copy(k).wait()
    detection = gain_ref[band] * coadd_ref[pl.ds(pl.multiple_of(band * share, EDGE), share), :]
    for k in range(1, bands):
        detection += gained_in[k].astype(jnp.float32)
    detection_ref[...] = detection

    for k in range(1, patches):
        near_back(k).wait()
    for k in range(patches):
        edge_back(k).wait()
    for k in range(1, patches):
        far_back(k).wait()

    @pl.loop(0, groups)
    def _(i):
        for g in range(group):
            t = i * group + g
            back = jnp.dot(
                turned_ref[t], low_ref[targets_ref[t, 0]], preferred_element_type=jnp.float32
            ).astype(jnp.bfloat16)
            template = jnp.dot(back, cols_ref[t], preferred_element_type=jnp.float32)
            template = template.astype(jnp.bfloat16).astype(jnp.float32)
            diff_ref[t] = (tiles_ref[t].astype(jnp.float32) - template).astype(jnp.bfloat16)
        out_copy(i).start()

    for i in range(groups):
        out_copy(i).wait()


def body(tiles, targets, offsets, fractions, kernels, weights, band_gain):
    holding, height, extent = tiles.shape[2:]
    patches, bands = lax.axis_size("patch"), lax.axis_size("band")
    images, target = tiles[0, 0], targets[0, 0]
    params = jnp.concatenate(
        [
            offsets[0, 0].astype(jnp.float32) + fractions[0, 0].astype(jnp.float32),
            kernels[0, 0].reshape(holding, 14).astype(jnp.float32),
            weights[0, 0][:, None].astype(jnp.float32),
        ],
        axis=1,
    )
    smem = pl.BlockSpec(memory_space=pltpu.SMEM)
    vmem = pl.BlockSpec(memory_space=pltpu.VMEM)
    anywhere = pl.BlockSpec(memory_space=pl.ANY)
    stored = pl.BlockSpec(memory_space=pltpu.HBM)
    group = 8
    padded = -(-patches // 8) * 8
    macs = holding * height * extent * extent
    share, half = height // bands, height // 2
    low, dma = jnp.bfloat16, pltpu.SemaphoreType.DMA
    per_patch = lambda rows: pltpu.VMEM((patches, rows, extent), low)
    coadd, detection, difference = pl.pallas_call(
        functools.partial(coadd_kernel, patches, bands, group),
        in_specs=[smem, smem, smem, stored],
        out_specs=[vmem, vmem, anywhere],
        out_shape=[
            jax.ShapeDtypeStruct((height, extent), jnp.float32),
            jax.ShapeDtypeStruct((share, extent), jnp.float32),
            jax.ShapeDtypeStruct((holding, height, extent), low),
        ],
        scratch_shapes=[
            pltpu.VMEM((holding, height, extent), low),
            pltpu.VMEM((holding, height, extent), low),
            pltpu.VMEM((holding, extent, extent), low),
            pltpu.VMEM((height + EDGE, holding * 128), low),
            pltpu.VMEM((holding, height, height + EDGE), low),
            pltpu.VMEM((holding * height, extent), low),
            pltpu.VMEM((padded, holding * 128), jnp.float32),
            pltpu.VMEM((padded, 128), jnp.float32),
            per_patch(half + EDGE),
            per_patch(EDGE),
            per_patch(half),
            per_patch(half + EDGE),
            per_patch(EDGE),
            per_patch(half),
            per_patch(height + EDGE),
            pltpu.VMEM((height, extent), low),
            pltpu.VMEM((bands, share, extent), low),
            dma((holding // group,)),
            dma((holding // group,)),
        ]
        + [dma((patches,))] * 12
        + [dma((bands,))] * 2,
        compiler_params=pltpu.CompilerParams(
            collective_id=0, has_side_effects=True, vmem_limit_bytes=48 << 20
        ),
        cost_estimate=pl.CostEstimate(flops=8 * macs, bytes_accessed=5 << 20, transcendentals=0),
        name="coadd",
    )(params, target, band_gain, images)
    return (coadd[None, None], detection[None], difference[None, None])


def solution(mesh):
    placed = (
        P(("tract", "band"), "patch", None, "row", None),
        P(("tract", "band"), "patch", None, None),
        P(("tract", "band"), "patch", None, None),
        P(("tract", "band"), "patch", None, None),
        P(("tract", "band"), "patch", None, None, None),
        P(("tract", "band"), "patch", None),
        P(),
    )
    return jax.shard_map(
        body,
        mesh=mesh,
        in_specs=placed,
        out_specs=(
            P(("tract", "band"), "patch", "row", None),
            P(("tract", "patch"), ("row", "band"), None),
            P(("tract", "band"), "patch", None, "row", None),
        ),
        check_vma=False,
    )
```

```python
import functools
import math

import jax
import jax.numpy as jnp
from jax import lax
from jax.experimental import pallas as pl
from jax.experimental.pallas import tpu as pltpu
from jax.sharding import PartitionSpec as P

EDGE = 16
MESH = pl.DeviceIdType.MESH


def lanczos(x):
    w = (x * x) * jnp.float32((math.pi / 3.0) ** 2)
    q = jnp.full_like(w, (-1.0) ** 10 / math.factorial(21))
    for k in range(9, -1, -1):
        q = q * w + jnp.float32((-1.0) ** k / math.factorial(2 * k + 1))
    q2 = q * q
    value = q2 * (1.0 - jnp.float32(4.0 / 3.0) * w * q2)
    return jnp.where(jnp.abs(x) < 3.0, value, 0.0)


def skewed(shift, taps):
    row = lax.broadcasted_iota(jnp.int32, (8, 128), 0)
    lane = lax.broadcasted_iota(jnp.int32, (8, 128), 1)
    lag = (lane - 64 - row).astype(jnp.float32)
    table = lanczos(lag - shift)
    mid = top = bottom = None
    for d in range(-3, 4):
        term = taps(d + 3) * (table if d == 0 else pltpu.roll(table, d % 128, 1))
        term_top = term if d >= 0 else jnp.where(row + d >= 0, term, 0.0)
        term_bottom = term if d <= 0 else jnp.where(row + d < 8, term, 0.0)
        mid = term if mid is None else mid + term
        top = term_top if top is None else top + term_top
        bottom = term_bottom if bottom is None else bottom + term_bottom
    return top, mid, bottom


def place(block, k):
    amount = (8 * k - 64) % 128
    return block if amount == 0 else pltpu.roll(block, amount, 1)


def low_half(block):
    lane = lax.broadcasted_iota(jnp.int32, block.shape, 1)
    return jnp.where(lane < 64, block, 0.0)


def high_half(block):
    lane = lax.broadcasted_iota(jnp.int32, block.shape, 1)
    return jnp.where(lane >= 64, block, 0.0)


def pair(first, second):
    return jnp.concatenate([first, second], axis=0).astype(jnp.bfloat16)


def build_columns(params_ref, t, put):
    top, mid, bottom = skewed(params_ref[0, t], lambda d: params_ref[2 + 2 * d, t])
    rolled = [place(mid, k) for k in range(16)]
    blocks = rolled + rolled
    blocks[0], blocks[31] = place(top, 0), place(bottom, 31)
    zero = jnp.zeros((16, 128), jnp.bfloat16)
    for q in range(16):
        both = blocks[2 * q], blocks[2 * q + 1]
        if q > 8:
            put(q, 0, zero)
        elif q in (7, 8):
            put(q, 0, pair(*[high_half(b) for b in both]))
        else:
            put(q, 0, pair(*[low_half(b) if q == 0 else b for b in both]))
        if q < 7:
            put(q, 1, zero)
        elif q in (7, 8):
            put(q, 1, pair(*[low_half(b) for b in both]))
        else:
            put(q, 1, pair(*[high_half(b) if q == 15 else b for b in both]))


def build_rows(params_ref, t, side, scale, put):
    top, mid, bottom = skewed(params_ref[1, t], lambda d: params_ref[3 + 2 * d, t])
    top, mid, bottom = top * scale, mid * scale, bottom * scale
    upper = side == 0
    first = jnp.where(upper, top, mid)
    last = jnp.where(upper, mid, bottom)
    blocks = [place(first, 0)] + [place(mid, k) for k in range(1, 15)] + [place(last, 15)]
    for q in range(8):
        both = blocks[2 * q], blocks[2 * q + 1]
        if q == 0:
            both = [low_half(b) for b in both]
        if q == 7:
            both = [high_half(b) for b in both]
        put(q, pair(*both))
    below = [high_half(place(mid, 16 + h)) for h in range(2)]
    above = [low_half(place(mid, h - 2)) for h in range(2)]
    put(8, pair(*[jnp.where(upper, b, a) for b, a in zip(below, above)]))


def coadd_kernel(
    patches, bands, group, offsets_ref, fractions_ref, kernels_ref, weights_ref, targets_ref, gain_ref,
    tiles_hbm,
    coadd_ref, detection_ref, low_ref, cols_hbm, turned_hbm,
    staged_ref, params_ref, params_sem, cols_ref, turned_ref, cols_sem, turned_sem, tiles_ref, rows_ref, section_ref, mask_ref, den_ref,
    near_out, edge_out, far_out, near_in, edge_in, far_in, gained_out, gained_in,
    tile_sem, near_send, near_recv, edge_send, edge_recv, far_send, far_recv,
    near_back_send, near_back_recv, edge_back_send, edge_back_recv, far_back_send, far_back_recv,
    band_send, band_recv,
):
    me = lax.axis_index("patch")
    band = lax.axis_index("band")
    side = lax.axis_index("row")
    holding, height = tiles_ref.shape[:2]
    share = detection_ref.shape[0]
    half = height // 2
    groups = holding // group
    across = 1 - side
    near_at = pl.multiple_of((1 - side) * half, EDGE)
    far_at = pl.multiple_of(side * half, EDGE)
    edge_at = pl.multiple_of((1 - side) * (half - EDGE), EDGE)

    def tile_copy(i):
        part = pl.ds(i * group, group)
        return pltpu.make_async_copy(tiles_hbm.at[part], tiles_ref.at[part], tile_sem.at[i])

    for i in range(groups):
        tile_copy(i).start()
    staged_ref[...] = jnp.zeros_like(staged_ref)
    staged_ref[0:2, :holding] = offsets_ref[...].astype(jnp.float32) + fractions_ref[...].astype(jnp.float32)
    for d in range(7):
        staged_ref[2 + 2 * d : 4 + 2 * d, :holding] = kernels_ref[d].astype(jnp.float32)
    staged_ref[16:17, :holding] = weights_ref[...].astype(jnp.float32)
    params_copy = pltpu.make_async_copy(staged_ref, params_ref, params_sem)
    params_copy.start()
    barrier = pltpu.get_barrier_semaphore()
    for k in range(1, patches):
        z = lax.rem(me + k, patches)
        pl.semaphore_signal(barrier, inc=1, device_id={"patch": z}, device_id_type=MESH)
    for k in range(patches):
        z = lax.rem(me + k, patches)
        pl.semaphore_signal(
            barrier, inc=1, device_id={"patch": z, "row": across}, device_id_type=MESH
        )
    for k in range(1, bands):
        b = lax.rem(band + k, bands)
        pl.semaphore_signal(barrier, inc=1, device_id={"band": b}, device_id_type=MESH)

    def remote(source, place_at, send, recv, where):
        return pltpu.make_async_remote_copy(
            src_ref=source, dst_ref=place_at, send_sem=send, recv_sem=recv,
            device_id=where, device_id_type=MESH,
        )

    params_copy.wait()
    den_ref[...] = jnp.zeros_like(den_ref)
    index = lax.broadcasted_iota(jnp.int32, den_ref.shape, 0)

    @pl.loop(0, groups)
    def _(i):
        tile_copy(i).wait()
        for g in range(group):
            t = i * group + g
            weight = params_ref[16, t]
            lanes = pl.ds(pl.multiple_of(t * 128, 128), 128)

            def put_col(q, part, tile):
                cols_ref[t, 16 * q : 16 * q + 16, 128 * part : 128 * part + 128] = tile

            def put_row(q, tile):
                if q == 8:
                    start = half
                elif q < 4:
                    start = 16 * q + (1 - side) * (half + EDGE)
                else:
                    start = 16 * (q - 4) + side * (half + EDGE)
                rows_ref[pl.ds(pl.multiple_of(start, EDGE), EDGE), lanes] = tile

            build_columns(params_ref, t, put_col)
            build_rows(params_ref, t, side, weight, put_row)
            section = lax.dot_general(
                tiles_ref[t], cols_ref[t], (((1,), (1,)), ((), ())), preferred_element_type=jnp.float32
            )
            section_ref[pl.ds(pl.multiple_of(t * height, height), height), :] = section.astype(jnp.bfloat16)
            chosen = index == targets_ref[0, t]
            mask_ref[:, lanes] = jnp.where(chosen, 1.0, 0.0)
            den_ref[...] += jnp.where(chosen, weight, 0.0)

    cols_copy = pltpu.make_async_copy(cols_ref, cols_hbm, cols_sem)
    turned_copy = pltpu.make_async_copy(turned_ref, turned_hbm, turned_sem)
    pl.semaphore_wait(barrier, 2 * patches - 1 + bands - 1)

    def near_copy(k):
        z = lax.rem(me + k, patches)
        return remote(near_out.at[k], near_in.at[k], near_send.at[k], near_recv.at[k], {"patch": z})

    def edge_copy(k):
        z = lax.rem(me + k, patches)
        return remote(
            edge_out.at[k], edge_in.at[k], edge_send.at[k], edge_recv.at[k], {"patch": z, "row": across}
        )

    def far_copy(k):
        z = lax.rem(me + k, patches)
        return remote(far_out.at[k], far_in.at[k], far_send.at[k], far_recv.at[k], {"patch": z})

    block = next(n for n in (4, 2, 1) if patches % n == 0)

    def patch_sums(first, start, size):
        rows = rows_ref[start : start + size]
        masked = []
        for j in range(block):
            z = lax.rem(me + first + j, patches)
            masked.append(rows * mask_ref[pl.ds(z, 1), :].astype(jnp.bfloat16))
        total = jnp.dot(
            jnp.concatenate(masked, axis=0), section_ref[...], preferred_element_type=jnp.float32
        ).astype(jnp.bfloat16)
        return [total[size * j : size * j + size] for j in range(block)]

    @pl.loop(0, patches // block)
    def _(i):
        for j, total in enumerate(patch_sums(i * block, 0, half + EDGE)):
            k = i * block + j
            near_out[k, :half] = total[:half]
            edge_out[k] = total[half:]
            den = den_ref[pl.ds(lax.rem(me + k, patches), 1), :]
            den = jnp.concatenate([den, den], axis=1)
            high = den.astype(jnp.bfloat16).astype(jnp.float32)
            line = lax.broadcasted_iota(jnp.int32, (EDGE, 256), 0)
            parts = jnp.where(line == 0, high, jnp.where(line == 1, den - high, 0.0))
            near_out[k, half:] = parts.astype(jnp.bfloat16)

    for k in range(1, patches):
        near_copy(k).start()
    for k in range(patches):
        edge_copy(k).start()

    @pl.loop(0, patches // block)
    def _(i):
        for j, total in enumerate(patch_sums(i * block, half + EDGE, half)):
            far_out[i * block + j] = total

    for k in range(1, patches):
        far_copy(k).start()

    cols_copy.start()

    def turn(t):
        lanes = pl.ds(pl.multiple_of(t * 128, 128), 128)
        block = rows_ref[:, lanes].astype(jnp.float32) * (1.0 / params_ref[16, t])
        turned_ref[t] = block.T.astype(jnp.bfloat16)

    @pl.loop(0, holding // 8)
    def _(i):
        for g in range(4):
            turn(i * 4 + g)

    for k in range(1, patches):
        near_copy(k).wait()
    for k in range(patches):
        edge_copy(k).wait()
    total = near_out[0].astype(jnp.float32)
    beside = edge_in[0].astype(jnp.float32)
    for k in range(1, patches):
        total += near_in[k].astype(jnp.float32)
        beside += edge_in[k].astype(jnp.float32)
    factor = 1.0 / (1.0 + jnp.sum(total[half:], axis=0, keepdims=True))
    zero = jnp.zeros((half - EDGE, 256), jnp.float32)
    beside = jnp.where(
        side == 0,
        jnp.concatenate([zero, beside], axis=0),
        jnp.concatenate([beside, zero], axis=0),
    )
    near = (total[:half] + beside) * factor
    low_ref[me, :half] = near.astype(jnp.bfloat16)

    def near_back(k):
        z = lax.rem(me + k, patches)
        here = low_ref.at[me, pl.ds(0, half)]
        return remote(here, here, near_back_send.at[k], near_back_recv.at[k], {"patch": z})

    def edge_back(k):
        z = lax.rem(me + k, patches)
        return remote(
            low_ref.at[me, pl.ds(edge_at, EDGE)], low_ref.at[me, pl.ds(half, EDGE)],
            edge_back_send.at[k], edge_back_recv.at[k], {"patch": z, "row": across},
        )

    def far_back(k):
        z = lax.rem(me + k, patches)
        here = low_ref.at[me, pl.ds(half + EDGE, half)]
        return remote(here, here, far_back_send.at[k], far_back_recv.at[k], {"patch": z})

    for k in range(1, patches):
        near_back(k).start()
    for k in range(patches):
        edge_back(k).start()
    coadd_ref[pl.ds(near_at, half), :] = near
    gained_out[pl.ds(near_at, half), :] = (gain_ref[band] * near).astype(jnp.bfloat16)

    for k in range(1, patches):
        far_copy(k).wait()
    far = far_out[0].astype(jnp.float32)
    for k in range(1, patches):
        far += far_in[k].astype(jnp.float32)
    far = far * factor
    low_ref[me, half + EDGE :] = far.astype(jnp.bfloat16)
    for k in range(1, patches):
        far_back(k).start()
    coadd_ref[pl.ds(far_at, half), :] = far
    gained_out[pl.ds(far_at, half), :] = (gain_ref[band] * far).astype(jnp.bfloat16)

    def band_copy(k):
        b = lax.rem(band + k, bands)
        return remote(
            gained_out.at[pl.ds(pl.multiple_of(b * share, EDGE), share)], gained_in.at[k],
            band_send.at[k], band_recv.at[k], {"band": b},
        )

    for k in range(1, bands):
        band_copy(k).start()

    @pl.loop(holding // 8, holding // 4)
    def _(i):
        for g in range(4):
            turn(i * 4 + g)

    turned_copy.start()
    for k in range(1, bands):
        band_copy(k).wait()
    detection = gain_ref[band] * coadd_ref[pl.ds(pl.multiple_of(band * share, EDGE), share), :]
    for k in range(1, bands):
        detection += gained_in[k].astype(jnp.float32)
    detection_ref[...] = detection

    for k in range(1, patches):
        near_back(k).wait()
    for k in range(patches):
        edge_back(k).wait()
    for k in range(1, patches):
        far_back(k).wait()
    cols_copy.wait()
    turned_copy.wait()


def template_kernel(
    group, targets_ref, tiles_hbm, low_ref, cols_hbm, turned_hbm, coadd_ref, detection_ref,
    coadd_out, detection_out, out_hbm, tiles_ref, cols_ref, turned_ref, diff_ref,
    coadd_sem, detection_sem, out_sem, tile_sem, cols_sem, turned_sem,
):
    groups = tiles_ref.shape[0] // group

    def out_copy(i):
        part = pl.ds(i * group, group)
        return pltpu.make_async_copy(diff_ref.at[part], out_hbm.at[part], out_sem.at[i])

    def in_copies(i):
        part = pl.ds(i * group, group)
        return (
            pltpu.make_async_copy(turned_hbm.at[part], turned_ref.at[part], turned_sem.at[i]),
            pltpu.make_async_copy(cols_hbm.at[part], cols_ref.at[part], cols_sem.at[i]),
            pltpu.make_async_copy(tiles_hbm.at[part], tiles_ref.at[part], tile_sem.at[i]),
        )

    for i in range(groups):
        for copy in in_copies(i):
            copy.start()
    coadd_copy = pltpu.make_async_copy(coadd_ref, coadd_out, coadd_sem)
    detection_copy = pltpu.make_async_copy(detection_ref, detection_out, detection_sem)
    coadd_copy.start()
    detection_copy.start()

    @pl.loop(0, groups)
    def _(i):
        for copy in in_copies(i):
            copy.wait()
        for g in range(group):
            t = i * group + g
            back = jnp.dot(
                turned_ref[t], low_ref[targets_ref[0, t]], preferred_element_type=jnp.float32
            ).astype(jnp.bfloat16)
            template = jnp.dot(back, cols_ref[t], preferred_element_type=jnp.float32)
            template = template.astype(jnp.bfloat16).astype(jnp.float32)
            diff_ref[t] = (tiles_ref[t].astype(jnp.float32) - template).astype(jnp.bfloat16)
        out_copy(i).start()

    for i in range(groups):
        out_copy(i).wait()
    coadd_copy.wait()
    detection_copy.wait()


def body(tiles, targets, offsets, fractions, kernels, weights, band_gain):
    holding, height, extent = tiles.shape[2:]
    patches, bands = lax.axis_size("patch"), lax.axis_size("band")
    images, target = tiles[0, 0], targets[0, 0, :, 0][None, :]
    smem = pl.BlockSpec(memory_space=pltpu.SMEM)
    vmem = pl.BlockSpec(memory_space=pltpu.VMEM)
    anywhere = pl.BlockSpec(memory_space=pl.ANY)
    group = 8
    padded = -(-patches // 8) * 8
    macs = holding * height * extent * extent
    share, half = height // bands, height // 2
    low, dma = jnp.bfloat16, pltpu.SemaphoreType.DMA
    per_patch = lambda rows: pltpu.VMEM((patches, rows, extent), low)
    coadd, detection, low_coadd, cols, turned = pl.pallas_call(
        functools.partial(coadd_kernel, patches, bands, group),
        in_specs=[vmem, vmem, vmem, vmem, smem, smem, anywhere],
        out_specs=[vmem, vmem, vmem, anywhere, anywhere],
        out_shape=[
            jax.ShapeDtypeStruct((height, extent), jnp.float32),
            jax.ShapeDtypeStruct((share, extent), jnp.float32),
            jax.ShapeDtypeStruct((patches, height + EDGE, extent), low),
            jax.ShapeDtypeStruct((holding, extent, extent), low),
            jax.ShapeDtypeStruct((holding, height, height + EDGE), low),
        ],
        scratch_shapes=[
            pltpu.VMEM((24, 128), jnp.float32),
            pltpu.SMEM((24, 128), jnp.float32),
            dma,
            pltpu.VMEM((holding, extent, extent), low),
            pltpu.VMEM((holding, height, height + EDGE), low),
            dma,
            dma,
            pltpu.VMEM((holding, height, extent), low),
            pltpu.VMEM((height + EDGE, holding * 128), low),
            pltpu.VMEM((holding * height, extent), low),
            pltpu.VMEM((padded, holding * 128), jnp.float32),
            pltpu.VMEM((padded, 128), jnp.float32),
            per_patch(half + EDGE),
            per_patch(EDGE),
            per_patch(half),
            per_patch(half + EDGE),
            per_patch(EDGE),
            per_patch(half),
            pltpu.VMEM((height, extent), low),
            pltpu.VMEM((bands, share, extent), low),
            dma((holding // group,)),
        ]
        + [dma((patches,))] * 12
        + [dma((bands,))] * 2,
        compiler_params=pltpu.CompilerParams(
            collective_id=0, has_side_effects=True, vmem_limit_bytes=60 << 20
        ),
        cost_estimate=pl.CostEstimate(flops=4 * macs, bytes_accessed=3 << 20, transcendentals=0),
        name="coadd",
    )(
        offsets[0, 0].T,
        fractions[0, 0].T,
        kernels[0, 0].transpose(2, 1, 0),
        weights[0, 0][None, :],
        target,
        band_gain,
        images,
    )
    coadd, detection, difference = pl.pallas_call(
        functools.partial(template_kernel, group),
        in_specs=[smem, anywhere, vmem, anywhere, anywhere, vmem, vmem],
        out_specs=[anywhere, anywhere, anywhere],
        out_shape=[
            jax.ShapeDtypeStruct((height, extent), jnp.float32),
            jax.ShapeDtypeStruct((share, extent), jnp.float32),
            jax.ShapeDtypeStruct((holding, height, extent), low),
        ],
        scratch_shapes=[
            pltpu.VMEM((holding, height, extent), low),
            pltpu.VMEM((holding, extent, extent), low),
            pltpu.VMEM((holding, height, height + EDGE), low),
            pltpu.VMEM((holding, height, extent), low),
            dma,
            dma,
        ]
        + [dma((holding // group,))] * 4,
        compiler_params=pltpu.CompilerParams(vmem_limit_bytes=60 << 20),
        cost_estimate=pl.CostEstimate(flops=4 * macs, bytes_accessed=3 << 20, transcendentals=0),
        name="templates",
    )(target, images, low_coadd, cols, turned, coadd, detection)
    return (coadd[None, None], detection[None], difference[None, None])


def solution(mesh):
    placed = (
        P(("tract", "band"), "patch", None, "row", None),
        P(("tract", "band"), "patch", None, None),
        P(("tract", "band"), "patch", None, None),
        P(("tract", "band"), "patch", None, None),
        P(("tract", "band"), "patch", None, None, None),
        P(("tract", "band"), "patch", None),
        P(),
    )
    return jax.shard_map(
        body,
        mesh=mesh,
        in_specs=placed,
        out_specs=(
            P(("tract", "band"), "patch", "row", None),
            P(("tract", "patch"), ("row", "band"), None),
            P(("tract", "band"), "patch", None, "row", None),
        ),
        check_vma=False,
    )
```
